256 devices in a mesh: gx: 16 (over y, x_hi, core), gy: 16 (over x_lo, z).
Axes of the slice: x: 4 (x_hi: 2, x_lo: 2; x = x_hi * 2 + x_lo), y: 4, z: 8, core: 2. Of those that a mesh axis runs over, the one named last changes fastest.
Arguments:
- east_flow: float32 [8, 2048, 8192], P(None, 'gx', 'gy'), may hold values from -36 to 36
- north_flow: float32 [8, 2048, 8192], P(None, 'gx', 'gy'), may hold values from -36 to 36
Outputs:
- stress: float32 [3, 8, 512, 2048], P(None, None, 'gx', 'gy')
- library: float32 [48, 8, 512, 2048], P(None, None, 'gx', 'gy')
The draws below stay inside these ranges and needn't reach their ends.
All inputs are finite; a program needn't handle non-finite values.
Results may differ from the reference program's by a relative error of at most 0.0003.
Values sent between devices are 32-bit elements; how exact they have to be, the bound alone decides.
A program may use at most 128 MiB of HBM per device.

```python
import jax
import jax.numpy as jnp
from jax import lax

LEV = 8
NX = 2048
NY = 8192


def shard_levels(own_key, dims, cuts, low, high):
    gain = 1.0
    for axis_at, parts in cuts:
        draws = jax.random.uniform(jax.random.fold_in(jax.random.fold_in(own_key, 6), axis_at), (parts,), jnp.float32, low / len(cuts), high / len(cuts))
        gain = gain * jnp.repeat(jnp.exp(draws), dims[axis_at] // parts).reshape((-1,) + (1,) * (len(dims) - 1 - axis_at))
    return gain


def bell_draw(key, dims, width, most, split=(), dtype=jnp.bfloat16):
    drawn = jax.random.normal(key, dims, jnp.float32) * width
    if len(split) > 0:
        drawn = shard_levels(key, dims, split, -0.22, 0.18) * drawn
    return jnp.clip(drawn, min=-most, max=most).astype(dtype)


def setup_inputs(seed: int = 0) -> dict:
    keys = jax.random.split(jax.random.key(seed), 3)
    return {
        "east_flow": bell_draw(keys[0], (LEV, NX, NY), 6.0, 36.0, ((1, 16), (2, 16)), jnp.float32),
        "north_flow": bell_draw(keys[1], (LEV, NX, NY), 6.0, 36.0, ((1, 16), (2, 16)), jnp.float32),
    }


spread_cells = 5.5


def gauss_taps():
    offsets = jnp.arange(33).astype(jnp.float32) - 16.0
    bumps = jnp.exp(-0.5 * (offsets / spread_cells) ** 2)
    return bumps / jnp.sum(bumps)


def coarse_smooth(field, weights):
    count_x, count_y = field.shape
    extended = jnp.concatenate([field[count_x - 16:], field, field[:16]], axis=0)
    rows_out = jnp.zeros((count_x // 4, count_y), jnp.float32)
    for offset in range(33):
        rows_out = rows_out + weights[offset] * extended[offset:offset + count_x:4]
    extended = jnp.concatenate([rows_out[:, count_y - 16:], rows_out, rows_out[:, :16]], axis=1)
    result = jnp.zeros((count_x // 4, count_y // 4), jnp.float32)
    for offset in range(33):
        result = result + weights[offset] * extended[:, offset:offset + count_y:4]
    return result


def first_form(plus_two, plus_one, minus_one, minus_two):
    return ((8.0 * plus_one - plus_two) - 8.0 * minus_one + minus_two) / 12.0


def second_form(plus_two, plus_one, centre, minus_one, minus_two):
    return (((16.0 * plus_one - plus_two) - 30.0 * centre) + 16.0 * minus_one - minus_two) / 12.0


def moved(field, step, axis):
    return jnp.roll(field, -step, axis)


def first_diff(field, axis):
    return first_form(moved(field, 2, axis), moved(field, 1, axis), moved(field, -1, axis), moved(field, -2, axis))


def second_diff(field, axis):
    return second_form(moved(field, 2, axis), moved(field, 1, axis), field, moved(field, -1, axis), moved(field, -2, axis))


def build_library(east_mean, north_mean, grad_ux, grad_uy, grad_vx, grad_vy, curve_uxx, curve_uxy, curve_uyy, curve_vxx, curve_vxy, curve_vyy):
    vorticity = grad_vx - grad_uy
    features = [grad_ux, grad_uy, grad_vx, grad_vy, curve_uxx, curve_uxy, curve_uyy, curve_vxx, curve_vxy, curve_vyy, curve_vxx - curve_uxy, curve_vxy - curve_uyy]
    columns = []
    for feature in features:
        columns.append(feature)
        columns.append(east_mean * feature)
        columns.append(north_mean * feature)
        columns.append(vorticity * feature)
    return jnp.stack(columns, axis=0)


def one_level(pair):
    east, north = pair
    weights = gauss_taps()
    means = [coarse_smooth(field, weights) for field in (east, north, east * east, east * north, north * north)]
    east_mean, north_mean = means[0], means[1]
    stress = jnp.stack([means[2] - east_mean * east_mean, means[3] - east_mean * north_mean, means[4] - north_mean * north_mean], axis=0)
    along_ux = first_diff(east_mean, 0)
    along_vx = first_diff(north_mean, 0)
    library = build_library(east_mean, north_mean, along_ux, first_diff(east_mean, 1), along_vx, first_diff(north_mean, 1),
                            second_diff(east_mean, 0), first_diff(along_ux, 1), second_diff(east_mean, 1),
                            second_diff(north_mean, 0), first_diff(along_vx, 1), second_diff(north_mean, 1))
    return stress, library


def reference(east_flow, north_flow):
    stress, library = lax.map(one_level, (east_flow, north_flow))
    return jnp.transpose(stress, (1, 0, 2, 3)), jnp.transpose(library, (1, 0, 2, 3))
```

```python
import jax
import jax.numpy as jnp
import ml_dtypes
import numpy as np
from jax import lax
from jax.experimental import pallas as pl
from jax.experimental.pallas import tpu as pltpu
from jax.sharding import PartitionSpec as P

spread_cells = 5.5
MESH = pl.DeviceIdType.MESH

LEV, FX, FY = 8, 128, 512
CX, CY = FX // 4, FY // 4
ROWS = CX + 8
PAIR = 2
CHUNKS = LEV // PAIR
COMBOS = 5 * PAIR
TILES = 8


def gauss_taps():
    offsets = np.arange(33, dtype=np.float32) - np.float32(16.0)
    bumps = np.exp(np.float32(-0.5) * (offsets / np.float32(spread_cells)) ** 2)
    return (bumps / np.sum(bumps)).astype(np.float32)


def two_pieces(values):
    high = values.astype(ml_dtypes.bfloat16)
    low = (values - high.astype(np.float32)).astype(ml_dtypes.bfloat16)
    return high, low


def row_factor():
    taps = gauss_taps()
    band = np.zeros((ROWS, FX), np.float32)
    for at in range(ROWS):
        for p in range(FX):
            lag = p - 4 * (at - 4) + 16
            if 0 <= lag <= 32:
                band[at, p] = taps[lag]
    high, low = two_pieces(band)
    return np.concatenate(
        [np.concatenate([high, high], axis=1), np.concatenate([low, low], axis=1)], axis=0
    )


def column_factor():
    taps = gauss_taps()
    half = FY // 2
    blocks = []
    for part in range(2):
        band = np.zeros((half, CY), np.float32)
        for c in range(-4, CY + 4):
            for p in range(half):
                lag = p + part * half - 4 * c + 16
                if 0 <= lag <= 32:
                    band[p, c % CY] = taps[lag]
        high, low = two_pieces(band)
        blocks.append(np.concatenate([high, low], axis=1))
    return np.stack(blocks, axis=0)


def split(values):
    high = values.astype(jnp.bfloat16)
    low = (values - high.astype(jnp.float32)).astype(jnp.bfloat16)
    return high, low


def turn(values, lanes):
    return pltpu.roll(values, lanes % CY, 1)


def filter_kernel(
    east, north, rows_hbm, cols_hbm, means, rims,
    fine, rows_w, cols_w, half_done, edges,
    to_y, to_x, from_y, from_c, from_x,
    load_sem, send_sem, recv_sem,
):
    here_x, here_y = lax.axis_index("gx"), lax.axis_index("gy")
    count_x, count_y = lax.axis_size("gx"), lax.axis_size("gy")
    up, down = lax.rem(here_x + 1, count_x), lax.rem(here_x + count_x - 1, count_x)
    right, left = lax.rem(here_y + 1, count_y), lax.rem(here_y + count_y - 1, count_y)
    neighbours = [
        (here_x, right), (here_x, left), (down, here_y), (up, here_y),
        (down, right), (up, right), (down, left), (up, left),
    ]

    barrier = pltpu.get_barrier_semaphore()
    for neighbour in neighbours:
        pl.semaphore_signal(barrier, inc=1, device_id=neighbour, device_id_type=MESH)

    def load(level, which):
        source = east if which == 0 else north
        return pltpu.make_async_copy(
            source.at[level], fine.at[which, level], load_sem.at[which, level]
        )

    rows_copy = pltpu.make_async_copy(rows_hbm, rows_w, load_sem.at[0, LEV])
    cols_copy = pltpu.make_async_copy(cols_hbm, cols_w, load_sem.at[1, LEV])
    rows_copy.start()
    load(0, 0).start()
    load(0, 1).start()
    cols_copy.start()

    def start_load(level, carry):
        load(level, 0).start()
        load(level, 1).start()
        return carry

    lax.fori_loop(1, LEV, start_load, 0)

    def sends(k):
        pieces = [
            (to_y.at[k, 0], from_y.at[k, 0]),
            (to_y.at[k, 1], from_y.at[k, 1]),
            (to_x.at[k, 0], from_x.at[k, 0]),
            (to_x.at[k, 1], from_x.at[k, 1]),
            (to_y.at[k, 0, pl.ds(0, 8)], from_c.at[k, 0]),
            (to_y.at[k, 0, pl.ds(CX, 8)], from_c.at[k, 1]),
            (to_y.at[k, 1, pl.ds(0, 8)], from_c.at[k, 2]),
            (to_y.at[k, 1, pl.ds(CX, 8)], from_c.at[k, 3]),
        ]
        return [
            pltpu.make_async_remote_copy(
                src_ref=source, dst_ref=target,
                send_sem=send_sem.at[k, n], recv_sem=recv_sem.at[k, n],
                device_id=neighbours[n], device_id_type=MESH,
            )
            for n, (source, target) in enumerate(pieces)
        ]

    rows_copy.wait()
    cols_copy.wait()
    pl.semaphore_wait(barrier, len(neighbours))

    lane = lax.broadcasted_iota(jnp.int32, (ROWS, CY), 1)
    group = lane // 8
    spot = lane % 8
    sub = lax.broadcasted_iota(jnp.int32, (8, CY), 0)

    def chunk(k, carry):
        for j in range(PAIR):
            level = PAIR * k + j
            load(level, 0).wait()
            load(level, 1).wait()
            u = fine[0, level]
            v = fine[1, level]
            for f, values in enumerate((u, v, u * u, u * v, v * v)):
                high, low = split(values)
                both = jnp.dot(
                    rows_w[...], jnp.concatenate([high, low], axis=0),
                    preferred_element_type=jnp.float32,
                )
                half_done[pl.ds((5 * j + f) * ROWS, ROWS), :] = both[:ROWS] + both[ROWS:]
        parts = []
        for part in range(2):
            high, low = split(half_done[:, part * (FY // 2):(part + 1) * (FY // 2)])
            weights = cols_w[part]
            both = jnp.dot(
                jnp.concatenate([high, low], axis=1),
                jnp.concatenate([weights, weights], axis=0),
                preferred_element_type=jnp.float32,
            )
            parts.append(both[:, :CY] + both[:, CY:])
        packed_main = jnp.zeros((ROWS, CY), jnp.float32)
        packed_edge = jnp.zeros((ROWS, CY), jnp.float32)
        for n in range(COMBOS):
            j, f = n // 5, n % 5
            first = parts[0][n * ROWS:(n + 1) * ROWS]
            second = parts[1][n * ROWS:(n + 1) * ROWS]
            main = jnp.where(lane < CY - 4, first, 0.0) + jnp.where(lane >= 4, second, 0.0)
            edge = jnp.where(lane >= CY // 2, first, second)
            means[PAIR * k + j, f] = main
            packed_edge = jnp.where(group == n, turn(edge, 8 * n + 4), packed_edge)
            if f < 2:
                packed_main = jnp.where(group == n, turn(main, 8 * n + 4), packed_main)
        edges[k] = packed_edge
        to_y[k, 0] = jnp.where(spot >= 4, packed_edge, packed_main)
        to_y[k, 1] = jnp.where(spot < 4, packed_edge, packed_main)
        for side in range(2):
            at = side * CX
            keep = (sub < 4) if side == 0 else (sub >= 4)

            def rows_of(j, f):
                return means[PAIR * k + j, f, pl.ds(at, 8)]

            for j in range(PAIR):
                to_x[k, side, 2 * j] = rows_of(j, 0)
                to_x[k, side, 2 * j + 1] = rows_of(j, 1)
                to_x[k, side, 4 + j] = jnp.where(
                    keep, rows_of(j, 2), pltpu.roll(rows_of(j, 3), 4, 0)
                )
            to_x[k, side, 6] = jnp.where(keep, rows_of(0, 4), pltpu.roll(rows_of(1, 4), 4, 0))
            to_x[k, side, 7] = packed_edge[at:at + 8]
        for copy in sends(k):
            copy.start()
        return carry

    lax.fori_loop(0, CHUNKS, chunk, 0)

    def join(k, carry):
        for copy in sends(k):
            copy.wait_recv()
        spans = ((0, 8), (8, CX - 8), (CX, 8))
        for at, size in spans:
            rows = pl.ds(at, size)
            from_left = from_y[k, 0, rows]
            from_right = from_y[k, 1, rows]
            own = edges[k, rows]
            if at == 0:
                from_left = from_left + from_c[k, 1]
                from_right = from_right + from_c[k, 3]
                own = own + from_x[k, 1, 7]
            if at == CX:
                from_left = from_left + from_c[k, 0]
                from_right = from_right + from_c[k, 2]
                own = own + from_x[k, 0, 7]
            near = spot[:size] >= 4
            inward = jnp.where(near, from_left, from_right)
            outward = jnp.where(near, from_right, from_left) + own
            lanes = lane[:size]
            inside = (lanes < 4) | (lanes >= CY - 4)
            for n in range(COMBOS):
                j, f = n // 5, n % 5
                level = PAIR * k + j
                total = means[level, f, rows] + jnp.where(inside, turn(inward, -8 * n - 4), 0.0)
                if at != 8:
                    side = 1 if at == 0 else 0
                    if f < 2:
                        total = total + from_x[k, side, 2 * j + f]
                    else:
                        slot = 4 + j if f < 4 else 6
                        tile = from_x[k, side, slot]
                        second_half = f == 3 or (f == 4 and j == 1)
                        total = total + (pltpu.roll(tile, 4, 0) if second_half else tile)
                means[level, f, rows] = total
                if f < 2:
                    rims[level, f, rows] = turn(outward, -8 * n - 4)
        return carry

    lax.fori_loop(0, CHUNKS, join, 0)

    def finish(k, carry):
        for copy in sends(k):
            copy.wait_send()
        return carry

    lax.fori_loop(0, CHUNKS, finish, 0)


def filtered(east_flow, north_flow):
    dma = pltpu.SemaphoreType.DMA
    anywhere = pl.BlockSpec(memory_space=pltpu.HBM)
    inside = pl.BlockSpec(memory_space=pltpu.VMEM)
    f32, bf16 = jnp.float32, jnp.bfloat16
    return pl.pallas_call(
        filter_kernel,
        out_shape=(
            jax.ShapeDtypeStruct((LEV, 5, ROWS, CY), f32),
            jax.ShapeDtypeStruct((LEV, 2, ROWS, CY), f32),
        ),
        in_specs=[anywhere] * 4,
        out_specs=(inside, inside),
        scratch_shapes=[
            pltpu.VMEM((2, LEV, FX, FY), f32),
            pltpu.VMEM((2 * ROWS, 2 * FX), bf16),
            pltpu.VMEM((2, FY // 2, 2 * CY), bf16),
            pltpu.VMEM((COMBOS * ROWS, FY), f32),
            pltpu.VMEM((CHUNKS, ROWS, CY), f32),
            pltpu.VMEM((CHUNKS, 2, ROWS, CY), f32),
            pltpu.VMEM((CHUNKS, 2, TILES, 8, CY), f32),
            pltpu.VMEM((CHUNKS, 2, ROWS, CY), f32),
            pltpu.VMEM((CHUNKS, 4, 8, CY), f32),
            pltpu.VMEM((CHUNKS, 2, TILES, 8, CY), f32),
            dma((2, LEV + 1)),
            dma((CHUNKS, 8)),
            dma((CHUNKS, 8)),
        ],
        compiler_params=pltpu.CompilerParams(
            collective_id=0, has_side_effects=True, vmem_limit_bytes=32 * 1024 * 1024
        ),
        name="filter_and_exchange",
    )(
        *[
            pltpu.with_memory_space_constraint(array, pltpu.HBM)
            for array in (
                east_flow, north_flow, jnp.asarray(row_factor()), jnp.asarray(column_factor())
            )
        ]
    )


def first_form(plus_two, plus_one, minus_one, minus_two):
    return (8.0 * (plus_one - minus_one) - (plus_two - minus_two)) * (1.0 / 12.0)


def second_form(plus_two, plus_one, centre, minus_one, minus_two):
    return (16.0 * (plus_one + minus_one) - (plus_two + minus_two) - 30.0 * centre) * (1.0 / 12.0)


def library_kernel(means, rims, stress, library, slopes):
    level = pl.program_id(0)
    lane = lax.broadcasted_iota(jnp.int32, (ROWS, CY), 1)
    results = []
    for f in range(2):
        field = means[level, f]
        rim = rims[level, f]
        near = [
            turn(jnp.where(lane < 2, rim, field), -2),
            turn(jnp.where(lane < 1, rim, field), -1),
            turn(jnp.where(lane >= CY - 1, rim, field), 1),
            turn(jnp.where(lane >= CY - 2, rim, field), 2),
        ]
        slopes[f] = first_form(*near)
        bend_y = second_form(near[0], near[1], field, near[2], near[3])[4:4 + CX]

        def row(step):
            return means[level, f, pl.ds(4 + step, CX)]

        def slope_row(step):
            return slopes[f, pl.ds(4 + step, CX)]

        centre = row(0)
        along = [row(2), row(1), row(-1), row(-2)]
        grad_x = first_form(*along)
        bend_x = second_form(along[0], along[1], centre, along[2], along[3])
        cross = first_form(slope_row(2), slope_row(1), slope_row(-1), slope_row(-2))
        results.append((centre, grad_x, slope_row(0), bend_x, cross, bend_y))
    east, ux, uy, uxx, uxy, uyy = results[0]
    north, vx, vy, vxx, vxy, vyy = results[1]
    stress[0, 0] = means[level, 2, pl.ds(4, CX)] - east * east
    stress[1, 0] = means[level, 3, pl.ds(4, CX)] - east * north
    stress[2, 0] = means[level, 4, pl.ds(4, CX)] - north * north
    spin = vx - uy
    features = [ux, uy, vx, vy, uxx, uxy, uyy, vxx, vxy, vyy, vxx - uxy, vxy - uyy]
    for n, feature in enumerate(features):
        library[4 * n, 0] = feature
        library[4 * n + 1, 0] = east * feature
        library[4 * n + 2, 0] = north * feature
        library[4 * n + 3, 0] = spin * feature


def outputs(means, rims):
    whole = pl.BlockSpec(memory_space=pltpu.VMEM)
    return pl.pallas_call(
        library_kernel,
        grid=(LEV,),
        out_shape=(
            jax.ShapeDtypeStruct((3, LEV, CX, CY), jnp.float32),
            jax.ShapeDtypeStruct((48, LEV, CX, CY), jnp.float32),
        ),
        in_specs=[whole, whole],
        out_specs=(
            pl.BlockSpec((3, 1, CX, CY), lambda l: (0, l, 0, 0)),
            pl.BlockSpec((48, 1, CX, CY), lambda l: (0, l, 0, 0)),
        ),
        scratch_shapes=[pltpu.VMEM((2, ROWS, CY), jnp.float32)],
        compiler_params=pltpu.CompilerParams(vmem_limit_bytes=32 * 1024 * 1024),
        name="stress_and_library",
    )(means, rims)


def per_device(east_flow, north_flow):
    means, rims = filtered(east_flow, north_flow)
    return outputs(means, rims)


def solution(mesh):
    return jax.shard_map(
        per_device,
        mesh=mesh,
        in_specs=(P(None, "gx", "gy"), P(None, "gx", "gy")),
        out_specs=(P(None, None, "gx", "gy"), P(None, None, "gx", "gy")),
        check_vma=False,
    )
```

```python
import jax
import jax.numpy as jnp
import ml_dtypes
import numpy as np
from jax import lax
from jax.experimental import pallas as pl
from jax.experimental.pallas import tpu as pltpu
from jax.sharding import PartitionSpec as P

spread_cells = 5.5
MESH = pl.DeviceIdType.MESH

LEV, FX, FY = 8, 128, 512
CX, CY = FX // 4, FY // 4
ROWS = CX + 8
PAIR = 2
CHUNKS = LEV // PAIR
COMBOS = 5 * PAIR
TILES = 8
AHEAD = 2


def gauss_taps():
    offsets = np.arange(33, dtype=np.float32) - np.float32(16.0)
    bumps = np.exp(np.float32(-0.5) * (offsets / np.float32(spread_cells)) ** 2)
    return (bumps / np.sum(bumps)).astype(np.float32)


def two_pieces(values):
    high = values.astype(ml_dtypes.bfloat16)
    low = (values - high.astype(np.float32)).astype(ml_dtypes.bfloat16)
    return high, low


def row_factor():
    taps = gauss_taps()
    band = np.zeros((ROWS, FX), np.float32)
    for at in range(ROWS):
        for p in range(FX):
            lag = p - 4 * (at - 4) + 16
            if 0 <= lag <= 32:
                band[at, p] = taps[lag]
    high, low = two_pieces(band)
    return np.concatenate(
        [np.concatenate([high, high], axis=1), np.concatenate([low, low], axis=1)], axis=0
    )


def column_factor():
    taps = gauss_taps()
    half = FY // 2
    blocks = []
    for part in range(2):
        band = np.zeros((half, CY), np.float32)
        for c in range(-4, CY + 4):
            for p in range(half):
                lag = p + part * half - 4 * c + 16
                if 0 <= lag <= 32:
                    band[p, c % CY] = taps[lag]
        high, low = two_pieces(band)
        blocks.append(np.concatenate([high, low], axis=1))
    return np.stack(blocks, axis=0)


def split(values):
    high = values.astype(jnp.bfloat16)
    low = (values - high.astype(jnp.float32)).astype(jnp.bfloat16)
    return high, low


def turn(values, lanes):
    return pltpu.roll(values, lanes % CY, 1)


def filter_kernel(
    east, north, rows_hbm, cols_hbm, means, edges, from_y, from_c, from_x,
    fine, rows_w, cols_w, half_done, to_y, to_x,
    load_sem, send_sem, recv_sem,
):
    def load(level, which):
        source = east if which == 0 else north
        return pltpu.make_async_copy(
            source.at[level], fine.at[which, level], load_sem.at[which, level]
        )

    rows_copy = pltpu.make_async_copy(rows_hbm, rows_w, load_sem.at[0, LEV])
    cols_copy = pltpu.make_async_copy(cols_hbm, cols_w, load_sem.at[1, LEV])
    load(0, 0).start()
    load(0, 1).start()
    rows_copy.start()
    cols_copy.start()
    for level in range(1, LEV):
        load(level, 0).start()
        load(level, 1).start()

    here_x, here_y = lax.axis_index("gx"), lax.axis_index("gy")
    count_x, count_y = lax.axis_size("gx"), lax.axis_size("gy")
    up, down = lax.rem(here_x + 1, count_x), lax.rem(here_x + count_x - 1, count_x)
    right, left = lax.rem(here_y + 1, count_y), lax.rem(here_y + count_y - 1, count_y)
    neighbours = [
        (down, here_y), (up, here_y), (here_x, right), (here_x, left),
        (down, right), (up, right), (down, left), (up, left),
    ]

    barrier = pltpu.get_barrier_semaphore()
    for neighbour in neighbours:
        pl.semaphore_signal(barrier, inc=1, device_id=neighbour, device_id_type=MESH)

    def sends(k):
        pieces = [
            (to_x.at[k, 0], from_x.at[k, 0]),
            (to_x.at[k, 1], from_x.at[k, 1]),
            (to_y.at[k, 0], from_y.at[k, 0]),
            (to_y.at[k, 1], from_y.at[k, 1]),
            (to_y.at[k, 0, pl.ds(0, 8)], from_c.at[k, 0]),
            (to_y.at[k, 0, pl.ds(CX, 8)], from_c.at[k, 1]),
            (to_y.at[k, 1, pl.ds(0, 8)], from_c.at[k, 2]),
            (to_y.at[k, 1, pl.ds(CX, 8)], from_c.at[k, 3]),
        ]
        return [
            pltpu.make_async_remote_copy(
                src_ref=source, dst_ref=target,
                send_sem=send_sem.at[k, n], recv_sem=recv_sem.at[k, n],
                device_id=neighbours[n], device_id_type=MESH,
            )
            for n, (source, target) in enumerate(pieces)
        ]

    def start_sends(k):
        for copy in sends(k):
            copy.start()

    rows_copy.wait()
    cols_copy.wait()

    lane = lax.broadcasted_iota(jnp.int32, (ROWS, CY), 1)
    group = lane // 8
    spot = lane % 8
    sub = lax.broadcasted_iota(jnp.int32, (8, CY), 0)

    def chunk(k):
        for j in range(PAIR):
            level = PAIR * k + j
            load(level, 0).wait()
            load(level, 1).wait()
            for half in range(2):
                at = pl.ds(half * (FY // 2), FY // 2)
                u = fine[0, level, :, at]
                v = fine[1, level, :, at]
                for f, values in enumerate((u, v, u * u, u * v, v * v)):
                    high, low = split(values)
                    both = jnp.dot(
                        rows_w[...], jnp.concatenate([high, low], axis=0),
                        preferred_element_type=jnp.float32,
                    )
                    half_done[pl.ds((5 * j + f) * ROWS, ROWS), at] = both[:ROWS] + both[ROWS:]
        parts = []
        for part in range(2):
            high, low = split(half_done[:, part * (FY // 2):(part + 1) * (FY // 2)])
            weights = cols_w[part]
            both = jnp.dot(
                jnp.concatenate([high, low], axis=1),
                jnp.concatenate([weights, weights], axis=0),
                preferred_element_type=jnp.float32,
            )
            parts.append(both[:, :CY] + both[:, CY:])
        packed_main = jnp.zeros((ROWS, CY), jnp.float32)
        packed_edge = jnp.zeros((ROWS, CY), jnp.float32)
        for n in range(COMBOS):
            j, f = n // 5, n % 5
            first = parts[0][n * ROWS:(n + 1) * ROWS]
            second = parts[1][n * ROWS:(n + 1) * ROWS]
            main = jnp.where(lane < CY - 4, first, 0.0) + jnp.where(lane >= 4, second, 0.0)
            edge = jnp.where(lane >= CY // 2, first, second)
            means[PAIR * k + j, f] = main
            packed_edge = jnp.where(group == n, turn(edge, 8 * n + 4), packed_edge)
            if f < 2:
                packed_main = jnp.where(group == n, turn(main, 8 * n + 4), packed_main)
        edges[k] = packed_edge
        to_y[k, 0] = jnp.where(spot >= 4, packed_edge, packed_main)
        to_y[k, 1] = jnp.where(spot < 4, packed_edge, packed_main)
        for side in range(2):
            at = side * CX
            keep = (sub < 4) if side == 0 else (sub >= 4)

            def rows_of(j, f):
                return means[PAIR * k + j, f, pl.ds(at, 8)]

            for j in range(PAIR):
                to_x[k, side, 2 * j] = rows_of(j, 0)
                to_x[k, side, 2 * j + 1] = rows_of(j, 1)
                to_x[k, side, 4 + j] = jnp.where(
                    keep, rows_of(j, 2), pltpu.roll(rows_of(j, 3), 4, 0)
                )
            to_x[k, side, 6] = jnp.where(keep, rows_of(0, 4), pltpu.roll(rows_of(1, 4), 4, 0))
            to_x[k, side, 7] = packed_edge[at:at + 8]

    def chunk_only(k, carry):
        chunk(k)
        return carry

    def chunk_and_send(k, carry):
        chunk(k)
        start_sends(k)
        return carry

    lax.fori_loop(0, AHEAD, chunk_only, 0)
    pl.semaphore_wait(barrier, len(neighbours))
    for k in range(AHEAD):
        start_sends(k)
    lax.fori_loop(AHEAD, CHUNKS, chunk_and_send, 0)

    def finish(k, carry):
        for copy in sends(k):
            copy.wait()
        return carry

    lax.fori_loop(0, CHUNKS, finish, 0)


def filtered(east_flow, north_flow):
    dma = pltpu.SemaphoreType.DMA
    f32, bf16 = jnp.float32, jnp.bfloat16
    shapes = (
        (LEV, 5, ROWS, CY), (CHUNKS, ROWS, CY),
        (CHUNKS, 2, ROWS, CY), (CHUNKS, 4, 8, CY), (CHUNKS, 2, TILES, 8, CY),
    )
    return pl.pallas_call(
        filter_kernel,
        out_shape=tuple(jax.ShapeDtypeStruct(shape, f32) for shape in shapes),
        in_specs=[pl.BlockSpec(memory_space=pltpu.HBM)] * 4,
        out_specs=(pl.BlockSpec(memory_space=pltpu.VMEM),) * len(shapes),
        scratch_shapes=[
            pltpu.VMEM((2, LEV, FX, FY), f32),
            pltpu.VMEM((2 * ROWS, 2 * FX), bf16),
            pltpu.VMEM((2, FY // 2, 2 * CY), bf16),
            pltpu.VMEM((COMBOS * ROWS, FY), f32),
            pltpu.VMEM((CHUNKS, 2, ROWS, CY), f32),
            pltpu.VMEM((CHUNKS, 2, TILES, 8, CY), f32),
            dma((2, LEV + 1)),
            dma((CHUNKS, 8)),
            dma((CHUNKS, 8)),
        ],
        compiler_params=pltpu.CompilerParams(
            collective_id=0, has_side_effects=True, vmem_limit_bytes=32 * 1024 * 1024
        ),
        name="filter_and_exchange",
    )(
        *[
            pltpu.with_memory_space_constraint(array, pltpu.HBM)
            for array in (
                east_flow, north_flow, jnp.asarray(row_factor()), jnp.asarray(column_factor())
            )
        ]
    )


def first_form(plus_two, plus_one, minus_one, minus_two):
    return (8.0 * (plus_one - minus_one) - (plus_two - minus_two)) * (1.0 / 12.0)


def second_form(plus_two, plus_one, centre, minus_one, minus_two):
    return (16.0 * (plus_one + minus_one) - (plus_two + minus_two) - 30.0 * centre) * (1.0 / 12.0)


def library_kernel(
    means, edges, from_y, from_c, from_x, stress, library, full, slopes, made_s, made_l, sem
):
    lane = lax.broadcasted_iota(jnp.int32, (ROWS, CY), 1)
    near = (lane % 8) >= 4
    inside = (lane < 4) | (lane >= CY - 4)

    def stores(level):
        return (
            pltpu.make_async_copy(made_s.at[level], stress.at[:, level], sem.at[0, level]),
            pltpu.make_async_copy(made_l.at[level], library.at[:, level], sem.at[1, level]),
        )

    def ends(first, last):
        middle = jnp.zeros((CX - 8, CY), jnp.float32)
        return jnp.concatenate([first, middle, last], axis=0)

    def chunk(k, carry):
        from_left = from_y[k, 0] + ends(from_c[k, 1], from_c[k, 0])
        from_right = from_y[k, 1] + ends(from_c[k, 3], from_c[k, 2])
        own = edges[k] + ends(from_x[k, 1, 7], from_x[k, 0, 7])
        inward = jnp.where(near, from_left, from_right)
        outward = jnp.where(near, from_right, from_left) + own
        for j in range(PAIR):
            level = PAIR * k + j
            for f in range(5):
                slot = 2 * j + f if f < 2 else (4 + j if f < 4 else 6)
                first, last = from_x[k, 1, slot], from_x[k, 0, slot]
                if f == 3 or (f == 4 and j == 1):
                    first, last = pltpu.roll(first, 4, 0), pltpu.roll(last, 4, 0)
                n = 5 * j + f
                full[f] = (
                    means[level, f]
                    + jnp.where(inside, turn(inward, -8 * n - 4), 0.0)
                    + ends(first, last)
                )
            results = []
            for f in range(2):
                field = full[f]
                rim = turn(outward, -8 * (5 * j + f) - 4)
                side = [
                    turn(jnp.where(lane < 2, rim, field), -2),
                    turn(jnp.where(lane < 1, rim, field), -1),
                    turn(jnp.where(lane >= CY - 1, rim, field), 1),
                    turn(jnp.where(lane >= CY - 2, rim, field), 2),
                ]
                slopes[f] = first_form(*side)
                bend_y = second_form(side[0], side[1], field, side[2], side[3])[4:4 + CX]

                def row(step):
                    return full[f, pl.ds(4 + step, CX)]

                def slope_row(step):
                    return slopes[f, pl.ds(4 + step, CX)]

                centre = row(0)
                along = [row(2), row(1), row(-1), row(-2)]
                grad_x = first_form(*along)
                bend_x = second_form(along[0], along[1], centre, along[2], along[3])
                cross = first_form(slope_row(2), slope_row(1), slope_row(-1), slope_row(-2))
                results.append((centre, grad_x, slope_row(0), bend_x, cross, bend_y))
            east, ux, uy, uxx, uxy, uyy = results[0]
            north, vx, vy, vxx, vxy, vyy = results[1]
            made_s[level, 0] = full[2, pl.ds(4, CX)] - east * east
            made_s[level, 1] = full[3, pl.ds(4, CX)] - east * north
            made_s[level, 2] = full[4, pl.ds(4, CX)] - north * north
            spin = vx - uy
            features = [ux, uy, vx, vy, uxx, uxy, uyy, vxx, vxy, vyy, vxx - uxy, vxy - uyy]
            for n, feature in enumerate(features):
                made_l[level, 4 * n] = feature
                made_l[level, 4 * n + 1] = east * feature
                made_l[level, 4 * n + 2] = north * feature
                made_l[level, 4 * n + 3] = spin * feature
            for copy in stores(level):
                copy.start()
        return carry

    lax.fori_loop(0, CHUNKS, chunk, 0)

    def finish(level, carry):
        for copy in stores(level):
            copy.wait()
        return carry

    lax.fori_loop(0, LEV, finish, 0)


def outputs(*arrays):
    f32 = jnp.float32
    return pl.pallas_call(
        library_kernel,
        out_shape=(
            jax.ShapeDtypeStruct((3, LEV, CX, CY), f32),
            jax.ShapeDtypeStruct((48, LEV, CX, CY), f32),
        ),
        in_specs=[pl.BlockSpec(memory_space=pltpu.VMEM)] * len(arrays),
        out_specs=(pl.BlockSpec(memory_space=pltpu.HBM),) * 2,
        scratch_shapes=[
            pltpu.VMEM((5, ROWS, CY), f32),
            pltpu.VMEM((2, ROWS, CY), f32),
            pltpu.VMEM((LEV, 3, CX, CY), f32),
            pltpu.VMEM((LEV, 48, CX, CY), f32),
            pltpu.SemaphoreType.DMA((2, LEV)),
        ],
        compiler_params=pltpu.CompilerParams(vmem_limit_bytes=32 * 1024 * 1024),
        name="stress_and_library",
    )(*arrays)


def per_device(east_flow, north_flow):
    return outputs(*filtered(east_flow, north_flow))


def solution(mesh):
    return jax.shard_map(
        per_device,
        mesh=mesh,
        in_specs=(P(None, "gx", "gy"), P(None, "gx", "gy")),
        out_specs=(P(None, None, "gx", "gy"), P(None, None, "gx", "gy")),
        check_vma=False,
    )
```

```python
import jax
import jax.numpy as jnp
import ml_dtypes
import numpy as np
from jax import lax
from jax.experimental import pallas as pl
from jax.experimental.pallas import tpu as pltpu
from jax.sharding import PartitionSpec as P

spread_cells = 5.5
MESH = pl.DeviceIdType.MESH

LEV, FX, FY = 8, 128, 512
CX, CY = FX // 4, FY // 4
ROWS = CX + 8
PAIR = 2
CHUNKS = LEV // PAIR
COMBOS = 5 * PAIR
TILES = 8
AHEAD = 0
EARLY_Z = 2


def gauss_taps():
    offsets = np.arange(33, dtype=np.float32) - np.float32(16.0)
    bumps = np.exp(np.float32(-0.5) * (offsets / np.float32(spread_cells)) ** 2)
    return (bumps / np.sum(bumps)).astype(np.float32)


def two_pieces(values):
    high = values.astype(ml_dtypes.bfloat16)
    low = (values - high.astype(np.float32)).astype(ml_dtypes.bfloat16)
    return high, low


def row_factor():
    taps = gauss_taps()
    band = np.zeros((ROWS, FX), np.float32)
    for at in range(ROWS):
        for p in range(FX):
            lag = p - 4 * (at - 4) + 16
            if 0 <= lag <= 32:
                band[at, p] = taps[lag]
    high, low = two_pieces(band)
    return np.concatenate(
        [np.concatenate([high, high], axis=1), np.concatenate([low, low], axis=1)], axis=0
    )


def column_factor():
    taps = gauss_taps()
    edge, half = FY // 4, FY // 2
    blocks = []
    for start, count in ((0, edge), (FY - edge, edge), (edge, half)):
        band = np.zeros((count, CY), np.float32)
        for c in range(-4, CY + 4):
            for p in range(count):
                lag = p + start - 4 * c + 16
                if 0 <= lag <= 32:
                    band[p, c % CY] = taps[lag]
        high, low = two_pieces(band)
        both = np.concatenate([high, low], axis=1)
        blocks.append(both if count == half else np.concatenate([both, both], axis=0))
    return np.stack(blocks, axis=0)


def split(values):
    high = values.astype(jnp.bfloat16)
    low = (values - high.astype(jnp.float32)).astype(jnp.bfloat16)
    return high, low


def turn(values, lanes):
    return pltpu.roll(values, lanes % CY, 1)


def filter_kernel(
    east, north, rows_hbm, cols_hbm, means, edges, from_y, from_c, from_x,
    sides, middle, rows_w, cols_w, half_done, to_y, to_x,
    load_sem, weight_sem, y_send, y_recv, x_send, x_recv,
):
    here_x, here_y = lax.axis_index("gx"), lax.axis_index("gy")
    count_x, count_y = lax.axis_size("gx"), lax.axis_size("gy")
    up, down = lax.rem(here_x + 1, count_x), lax.rem(here_x + count_x - 1, count_x)
    right, left = lax.rem(here_y + 1, count_y), lax.rem(here_y + count_y - 1, count_y)
    corners = [(down, right), (up, right), (down, left), (up, left)]
    along_y = [(here_x, right), (here_x, left)]
    along_x = [(down, here_y), (up, here_y)]
    neighbours = corners + along_y + along_x

    barrier = pltpu.get_barrier_semaphore()
    for neighbour in neighbours:
        pl.semaphore_signal(barrier, inc=1, device_id=neighbour, device_id_type=MESH)

    quarter = FY // 4

    def load(k, which, piece):
        source = (east if which == 0 else north).at[pl.ds(PAIR * k, PAIR)]
        levels = pl.ds(PAIR * k, PAIR)
        if piece == 0:
            source = source.at[:, :, pl.ds(0, quarter)]
            target = sides.at[which, levels, :, pl.ds(0, quarter)]
        elif piece == 1:
            source = source.at[:, :, pl.ds(3 * quarter, quarter)]
            target = sides.at[which, levels, :, pl.ds(quarter, quarter)]
        else:
            source = source.at[:, :, pl.ds(quarter, 2 * quarter)]
            target = middle.at[which, levels]
        return pltpu.make_async_copy(source, target, load_sem.at[k, which, piece])

    def start_loads(k, pieces):
        for which in range(2):
            for piece in pieces:
                load(k, which, piece).start()

    def wait_loads(k, pieces):
        for which in range(2):
            for piece in pieces:
                load(k, which, piece).wait()

    rows_copy = pltpu.make_async_copy(rows_hbm, rows_w, weight_sem.at[0])
    cols_copy = pltpu.make_async_copy(cols_hbm, cols_w, weight_sem.at[1])
    start_loads(0, (0, 1))
    rows_copy.start()
    cols_copy.start()
    for k in range(1, CHUNKS):
        start_loads(k, (0, 1))
    for k in range(CHUNKS):
        start_loads(k, (2,))

    def remote(source, target, send, recv, device):
        return pltpu.make_async_remote_copy(
            src_ref=source, dst_ref=target, send_sem=send, recv_sem=recv,
            device_id=device, device_id_type=MESH,
        )

    def sends_y():
        last = ROWS // 8 - 1
        pieces = [
            (to_y.at[0, 0], from_c.at[0]),
            (to_y.at[0, last], from_c.at[1]),
            (to_y.at[1, 0], from_c.at[2]),
            (to_y.at[1, last], from_c.at[3]),
            (to_y.at[0], from_y.at[0]),
            (to_y.at[1], from_y.at[1]),
        ]
        return [
            remote(source, target, y_send.at[n], y_recv.at[n], neighbours[n])
            for n, (source, target) in enumerate(pieces)
        ]

    def sends_x(k):
        return [
            remote(
                to_x.at[k, n], from_x.at[k, n], x_send.at[k, n], x_recv.at[k, n], along_x[n]
            )
            for n in range(2)
        ]

    rows_copy.wait()
    cols_copy.wait()

    lane = lax.broadcasted_iota(jnp.int32, (ROWS, CY), 1)
    group = lane // 8
    spot = lane % 8
    sub = lax.broadcasted_iota(jnp.int32, (8, CY), 0)

    def rows_first(k, fine):
        for j in range(PAIR):
            level = PAIR * k + j
            u = fine[0, level]
            v = fine[1, level]
            for f, values in enumerate((u, v, u * u, u * v, v * v)):
                high, low = split(values)
                both = jnp.dot(
                    rows_w[...], jnp.concatenate([high, low], axis=0),
                    preferred_element_type=jnp.float32,
                )
                half_done[pl.ds((5 * j + f) * ROWS, ROWS), :] = both[:ROWS] + both[ROWS:]

    def columns(values, weights):
        high, low = split(values)
        both = jnp.dot(
            jnp.concatenate([high, low], axis=1), weights, preferred_element_type=jnp.float32
        )
        return both[:, :CY] + both[:, CY:]

    def side_chunk(k, carry):
        wait_loads(k, (0, 1))
        rows_first(k, sides)
        from_low = columns(half_done[:, :quarter], cols_w[0])
        from_high = columns(half_done[:, quarter:], cols_w[1])
        packed_main = jnp.zeros((ROWS, CY), jnp.float32)
        packed_edge = jnp.zeros((ROWS, CY), jnp.float32)
        for n in range(COMBOS):
            j, f = n // 5, n % 5
            first = from_low[n * ROWS:(n + 1) * ROWS]
            second = from_high[n * ROWS:(n + 1) * ROWS]
            main = jnp.where(lane < CY - 4, first, 0.0) + jnp.where(lane >= 4, second, 0.0)
            edge = jnp.where(lane >= CY // 2, first, second)
            means[PAIR * k + j, f] = main
            packed_edge = jnp.where(group == n, turn(edge, 8 * n + 4), packed_edge)
            if f < 2:
                packed_main = jnp.where(group == n, turn(main, 8 * n + 4), packed_main)
        edges[k] = packed_edge
        at = pl.ds(8 * k, 8)
        tiled = (ROWS // 8, 8, CY)
        to_y[0, :, at] = jnp.where(spot >= 4, packed_edge, packed_main).reshape(tiled)
        to_y[1, :, at] = jnp.where(spot < 4, packed_edge, packed_main).reshape(tiled)
        return carry

    def middle_chunk(k):
        wait_loads(k, (2,))
        rows_first(k, middle)
        inner = columns(half_done[...], jnp.concatenate([cols_w[2], cols_w[2]], axis=0))
        for n in range(COMBOS):
            j, f = n // 5, n % 5
            means[PAIR * k + j, f] += inner[n * ROWS:(n + 1) * ROWS]
        for side in range(2):
            at = side * CX
            keep = (sub < 4) if side == 0 else (sub >= 4)

            def rows_of(j, f):
                return means[PAIR * k + j, f, pl.ds(at, 8)]

            for j in range(PAIR):
                to_x[k, side, 2 * j] = rows_of(j, 0)
                to_x[k, side, 2 * j + 1] = rows_of(j, 1)
                to_x[k, side, 4 + j] = jnp.where(
                    keep, rows_of(j, 2), pltpu.roll(rows_of(j, 3), 4, 0)
                )
            to_x[k, side, 6] = jnp.where(keep, rows_of(0, 4), pltpu.roll(rows_of(1, 4), 4, 0))
            to_x[k, side, 7] = edges[k, pl.ds(at, 8)]

    def middle_only(k, carry):
        middle_chunk(k)
        return carry

    def middle_and_send(k, carry):
        middle_chunk(k)
        for copy in sends_x(k):
            copy.start()
        return carry

    def send_only(k, carry):
        for copy in sends_x(k):
            copy.start()
        return carry

    ahead = jnp.where(lax.rem(here_y, 8) < EARLY_Z, CHUNKS, AHEAD)
    lax.fori_loop(0, CHUNKS, side_chunk, 0)
    lax.fori_loop(0, ahead, middle_only, 0)
    pl.semaphore_wait(barrier, len(neighbours))
    for copy in sends_y():
        copy.start()
    lax.fori_loop(0, ahead, send_only, 0)
    lax.fori_loop(ahead, CHUNKS, middle_and_send, 0)

    for k in range(CHUNKS):
        for copy in sends_x(k):
            copy.wait()
    for copy in sends_y():
        copy.wait()


def filtered(east_flow, north_flow):
    dma = pltpu.SemaphoreType.DMA
    f32, bf16 = jnp.float32, jnp.bfloat16
    tiles = ROWS // 8
    shapes = (
        (LEV, 5, ROWS, CY), (CHUNKS, ROWS, CY),
        (2, tiles, CHUNKS * 8, CY), (4, CHUNKS * 8, CY), (CHUNKS, 2, TILES, 8, CY),
    )
    return pl.pallas_call(
        filter_kernel,
        out_shape=tuple(jax.ShapeDtypeStruct(shape, f32) for shape in shapes),
        in_specs=[pl.BlockSpec(memory_space=pltpu.HBM)] * 4,
        out_specs=(pl.BlockSpec(memory_space=pltpu.VMEM),) * len(shapes),
        scratch_shapes=[
            pltpu.VMEM((2, LEV, FX, FY // 2), f32),
            pltpu.VMEM((2, LEV, FX, FY // 2), f32),
            pltpu.VMEM((2 * ROWS, 2 * FX), bf16),
            pltpu.VMEM((3, FY // 2, 2 * CY), bf16),
            pltpu.VMEM((COMBOS * ROWS, FY // 2), f32),
            pltpu.VMEM((2, tiles, CHUNKS * 8, CY), f32),
            pltpu.VMEM((CHUNKS, 2, TILES, 8, CY), f32),
            dma((CHUNKS, 2, 3)),
            dma((2,)),
            dma((6,)),
            dma((6,)),
            dma((CHUNKS, 2)),
            dma((CHUNKS, 2)),
        ],
        compiler_params=pltpu.CompilerParams(
            collective_id=0, has_side_effects=True, vmem_limit_bytes=32 * 1024 * 1024
        ),
        name="filter_and_exchange",
    )(
        *[
            pltpu.with_memory_space_constraint(array, pltpu.HBM)
            for array in (
                east_flow, north_flow, jnp.asarray(row_factor()), jnp.asarray(column_factor())
            )
        ]
    )


def first_form(plus_two, plus_one, minus_one, minus_two):
    return (8.0 * (plus_one - minus_one) - (plus_two - minus_two)) * (1.0 / 12.0)


def second_form(plus_two, plus_one, centre, minus_one, minus_two):
    return (16.0 * (plus_one + minus_one) - (plus_two + minus_two) - 30.0 * centre) * (1.0 / 12.0)


def library_kernel(
    means, edges, from_y, from_c, from_x, stress, library, full, slopes, made_s, made_l, sem
):
    lane = lax.broadcasted_iota(jnp.int32, (ROWS, CY), 1)
    near = (lane % 8) >= 4
    inside = (lane < 4) | (lane >= CY - 4)

    def stores(level):
        return (
            pltpu.make_async_copy(made_s.at[level], stress.at[:, level], sem.at[0, level]),
            pltpu.make_async_copy(made_l.at[level], library.at[:, level], sem.at[1, level]),
        )

    def ends(first, last):
        middle = jnp.zeros((CX - 8, CY), jnp.float32)
        return jnp.concatenate([first, middle, last], axis=0)

    def chunk(k, carry):
        at = pl.ds(8 * k, 8)
        from_left = from_y[0, :, at].reshape(ROWS, CY) + ends(from_c[1, at], from_c[0, at])
        from_right = from_y[1, :, at].reshape(ROWS, CY) + ends(from_c[3, at], from_c[2, at])
        own = edges[k] + ends(from_x[k, 1, 7], from_x[k, 0, 7])
        inward = jnp.where(near, from_left, from_right)
        outward = jnp.where(near, from_right, from_left) + own
        for j in range(PAIR):
            level = PAIR * k + j
            for f in range(5):
                slot = 2 * j + f if f < 2 else (4 + j if f < 4 else 6)
                first, last = from_x[k, 1, slot], from_x[k, 0, slot]
                if f == 3 or (f == 4 and j == 1):
                    first, last = pltpu.roll(first, 4, 0), pltpu.roll(last, 4, 0)
                n = 5 * j + f
                full[f] = (
                    means[level, f]
                    + jnp.where(inside, turn(inward, -8 * n - 4), 0.0)
                    + ends(first, last)
                )
            results = []
            for f in range(2):
                field = full[f]
                rim = turn(outward, -8 * (5 * j + f) - 4)
                side = [
                    turn(jnp.where(lane < 2, rim, field), -2),
                    turn(jnp.where(lane < 1, rim, field), -1),
                    turn(jnp.where(lane >= CY - 1, rim, field), 1),
                    turn(jnp.where(lane >= CY - 2, rim, field), 2),
                ]
                slopes[f] = first_form(*side)
                bend_y = second_form(side[0], side[1], field, side[2], side[3])[4:4 + CX]

                def row(step):
                    return full[f, pl.ds(4 + step, CX)]

                def slope_row(step):
                    return slopes[f, pl.ds(4 + step, CX)]

                centre = row(0)
                along = [row(2), row(1), row(-1), row(-2)]
                grad_x = first_form(*along)
                bend_x = second_form(along[0], along[1], centre, along[2], along[3])
                cross = first_form(slope_row(2), slope_row(1), slope_row(-1), slope_row(-2))
                results.append((centre, grad_x, slope_row(0), bend_x, cross, bend_y))
            east, ux, uy, uxx, uxy, uyy = results[0]
            north, vx, vy, vxx, vxy, vyy = results[1]
            made_s[level, 0] = full[2, pl.ds(4, CX)] - east * east
            made_s[level, 1] = full[3, pl.ds(4, CX)] - east * north
            made_s[level, 2] = full[4, pl.ds(4, CX)] - north * north
            spin = vx - uy
            features = [ux, uy, vx, vy, uxx, uxy, uyy, vxx, vxy, vyy, vxx - uxy, vxy - uyy]
            for n, feature in enumerate(features):
                made_l[level, 4 * n] = feature
                made_l[level, 4 * n + 1] = east * feature
                made_l[level, 4 * n + 2] = north * feature
                made_l[level, 4 * n + 3] = spin * feature
            for copy in stores(level):
                copy.start()
        return carry

    lax.fori_loop(0, CHUNKS, chunk, 0)

    def finish(level, carry):
        for copy in stores(level):
            copy.wait()
        return carry

    lax.fori_loop(0, LEV, finish, 0)


def outputs(*arrays):
    f32 = jnp.float32
    return pl.pallas_call(
        library_kernel,
        out_shape=(
            jax.ShapeDtypeStruct((3, LEV, CX, CY), f32),
            jax.ShapeDtypeStruct((48, LEV, CX, CY), f32),
        ),
        in_specs=[pl.BlockSpec(memory_space=pltpu.VMEM)] * len(arrays),
        out_specs=(pl.BlockSpec(memory_space=pltpu.HBM),) * 2,
        scratch_shapes=[
            pltpu.VMEM((5, ROWS, CY), f32),
            pltpu.VMEM((2, ROWS, CY), f32),
            pltpu.VMEM((LEV, 3, CX, CY), f32),
            pltpu.VMEM((LEV, 48, CX, CY), f32),
            pltpu.SemaphoreType.DMA((2, LEV)),
        ],
        compiler_params=pltpu.CompilerParams(vmem_limit_bytes=32 * 1024 * 1024),
        name="stress_and_library",
    )(*arrays)


def per_device(east_flow, north_flow):
    return outputs(*filtered(east_flow, north_flow))


def solution(mesh):
    return jax.shard_map(
        per_device,
        mesh=mesh,
        in_specs=(P(None, "gx", "gy"), P(None, "gx", "gy")),
        out_specs=(P(None, None, "gx", "gy"), P(None, None, "gx", "gy")),
        check_vma=False,
    )
```

```python
import jax
import jax.numpy as jnp
import ml_dtypes
import numpy as np
from jax import lax
from jax.experimental import pallas as pl
from jax.experimental.pallas import tpu as pltpu
from jax.sharding import PartitionSpec as P

spread_cells = 5.5
MESH = pl.DeviceIdType.MESH

LEV, FX, FY = 8, 128, 512
CX, CY = FX // 4, FY // 4
ROWS = CX + 8
PAIR = 2
CHUNKS = LEV // PAIR
COMBOS = 5 * PAIR
TILES = 6
AHEAD = 1


def slot_of(j, f):
    return 2 * j + f if f < 2 else 4 + 3 * j + f - 2


def gauss_taps():
    offsets = np.arange(33, dtype=np.float32) - np.float32(16.0)
    bumps = np.exp(np.float32(-0.5) * (offsets / np.float32(spread_cells)) ** 2)
    return (bumps / np.sum(bumps)).astype(np.float32)


def two_pieces(values):
    high = values.astype(ml_dtypes.bfloat16)
    low = (values - high.astype(np.float32)).astype(ml_dtypes.bfloat16)
    return high, low


def row_factor():
    taps = gauss_taps()
    band = np.zeros((ROWS, FX), np.float32)
    for at in range(ROWS):
        for p in range(FX):
            lag = p - 4 * (at - 4) + 16
            if 0 <= lag <= 32:
                band[at, p] = taps[lag]
    high, low = two_pieces(band)
    return np.concatenate(
        [np.concatenate([high, high], axis=1), np.concatenate([low, low], axis=1)], axis=0
    )


def column_factor():
    taps = gauss_taps()
    edge, half = FY // 4, FY // 2
    blocks = []
    for start, count in ((0, edge), (FY - edge, edge), (edge, half)):
        band = np.zeros((count, CY), np.float32)
        for c in range(-4, CY + 4):
            for p in range(count):
                lag = p + start - 4 * c + 16
                if 0 <= lag <= 32:
                    band[p, c % CY] = taps[lag]
        high, low = two_pieces(band)
        both = np.concatenate([high, low], axis=1)
        blocks.append(both if count == half else np.concatenate([both, both], axis=0))
    return np.stack(blocks, axis=0)


def split(values):
    high = values.astype(jnp.bfloat16)
    low = (values - high.astype(jnp.float32)).astype(jnp.bfloat16)
    return high, low


def turn(values, lanes):
    return pltpu.roll(values, lanes % CY, 1)


def filter_kernel(
    east, north, rows_hbm, cols_hbm, means, edges, from_y, from_c, from_x, from_e,
    sides, middle, rows_w, cols_w, half_done, to_y, to_x, to_e,
    load_sem, weight_sem, y_send, y_recv, x_send, x_recv,
):
    quarter = FY // 4

    def load(k, which, piece):
        source = (east if which == 0 else north).at[pl.ds(PAIR * k, PAIR)]
        levels = pl.ds(PAIR * k, PAIR)
        if piece == 0:
            source = source.at[:, :, pl.ds(0, quarter)]
            target = sides.at[which, levels, :, pl.ds(0, quarter)]
        elif piece == 1:
            source = source.at[:, :, pl.ds(3 * quarter, quarter)]
            target = sides.at[which, levels, :, pl.ds(quarter, quarter)]
        else:
            source = source.at[:, :, pl.ds(quarter, 2 * quarter)]
            target = middle.at[which, levels]
        return pltpu.make_async_copy(source, target, load_sem.at[k, which, piece])

    def start_loads(k, pieces):
        for which in range(2):
            for piece in pieces:
                load(k, which, piece).start()

    def wait_loads(k, pieces):
        for which in range(2):
            for piece in pieces:
                load(k, which, piece).wait()

    rows_copy = pltpu.make_async_copy(rows_hbm, rows_w, weight_sem.at[0])
    cols_copy = pltpu.make_async_copy(cols_hbm, cols_w, weight_sem.at[1])
    start_loads(0, (0, 1))
    rows_copy.start()
    cols_copy.start()
    here_x, here_y = lax.axis_index("gx"), lax.axis_index("gy")
    count_x, count_y = lax.axis_size("gx"), lax.axis_size("gy")
    up = jnp.where(here_x == count_x - 1, 0, here_x + 1)
    down = jnp.where(here_x == 0, count_x - 1, here_x - 1)
    right = jnp.where(here_y == count_y - 1, 0, here_y + 1)
    left = jnp.where(here_y == 0, count_y - 1, here_y - 1)
    corners = [(down, right), (up, right), (down, left), (up, left)]
    along_y = [(here_x, right), (here_x, left)]
    along_x = [(down, here_y), (up, here_y)]
    neighbours = corners + along_y + along_x

    barrier = pltpu.get_barrier_semaphore()
    for neighbour in neighbours:
        pl.semaphore_signal(barrier, inc=1, device_id=neighbour, device_id_type=MESH)

    for k in range(1, CHUNKS):
        start_loads(k, (0, 1))
    for k in range(CHUNKS):
        start_loads(k, (2,))

    def remote(source, target, send, recv, device):
        return pltpu.make_async_remote_copy(
            src_ref=source, dst_ref=target, send_sem=send, recv_sem=recv,
            device_id=device, device_id_type=MESH,
        )

    def sends_y():
        last = ROWS // 8 - 1
        pieces = [
            (to_y.at[0, 0], from_c.at[0]),
            (to_y.at[0, last], from_c.at[1]),
            (to_y.at[1, 0], from_c.at[2]),
            (to_y.at[1, last], from_c.at[3]),
            (to_y.at[0], from_y.at[0]),
            (to_y.at[1], from_y.at[1]),
            (to_e.at[0], from_e.at[0]),
            (to_e.at[1], from_e.at[1]),
        ]
        return [
            remote(source, target, y_send.at[n], y_recv.at[n], neighbours[n])
            for n, (source, target) in enumerate(pieces)
        ]

    def sends_x(k):
        return [
            remote(
                to_x.at[k, n], from_x.at[k, n], x_send.at[k, n], x_recv.at[k, n], along_x[n]
            )
            for n in range(2)
        ]

    rows_copy.wait()
    cols_copy.wait()

    lane = lax.broadcasted_iota(jnp.int32, (ROWS, CY), 1)
    group = lane // 8
    spot = lane % 8
    sub = lax.broadcasted_iota(jnp.int32, (8, CY), 0)

    def rows_first(k, fine):
        for j in range(PAIR):
            level = PAIR * k + j
            u = fine[0, level]
            v = fine[1, level]
            for f, values in enumerate((u, v, u * u, u * v, v * v)):
                high, low = split(values)
                both = jnp.dot(
                    rows_w[...], jnp.concatenate([high, low], axis=0),
                    preferred_element_type=jnp.float32,
                )
                half_done[pl.ds((5 * j + f) * ROWS, ROWS), :] = both[:ROWS] + both[ROWS:]

    def columns(values, weights):
        high, low = split(values)
        both = jnp.dot(
            jnp.concatenate([high, low], axis=1), weights, preferred_element_type=jnp.float32
        )
        return both[:, :CY] + both[:, CY:]

    def side_chunk(k, carry):
        wait_loads(k, (0, 1))
        rows_first(k, sides)
        from_low = columns(half_done[:, :quarter], cols_w[0])
        from_high = columns(half_done[:, quarter:], cols_w[1])
        packed_main = jnp.zeros((ROWS, CY), jnp.float32)
        packed_edge = jnp.zeros((ROWS, CY), jnp.float32)
        for at in range(COMBOS):
            j, f = at // 5, at % 5
            n = slot_of(j, f)
            first = from_low[at * ROWS:(at + 1) * ROWS]
            second = from_high[at * ROWS:(at + 1) * ROWS]
            main = jnp.where(lane < CY - 4, first, 0.0) + jnp.where(lane >= 4, second, 0.0)
            edge = jnp.where(lane >= CY // 2, first, second)
            means[PAIR * k + j, f] = main
            packed_edge = jnp.where(group == n, turn(edge, 8 * n + 4), packed_edge)
            if f < 2:
                packed_main = jnp.where(group == n, turn(main, 8 * n + 4), packed_main)
        edges[k] = packed_edge
        at = pl.ds(8 * k, 8)
        tiled = (ROWS // 8, 8, CY)
        quarter_lanes = lax.broadcasted_iota(jnp.int32, (8, CY), 1) // 32
        for side in range(2):
            turned = pltpu.roll(packed_edge[side * CX:side * CX + 8], 32 * k, 1)
            to_e[side] = jnp.where(quarter_lanes == k, turned, to_e[side])
        to_y[0, :, at] = jnp.where(spot >= 4, packed_edge, packed_main).reshape(tiled)
        to_y[1, :, at] = jnp.where(spot < 4, packed_edge, packed_main).reshape(tiled)
        return carry

    def middle_chunk(k):
        wait_loads(k, (2,))
        rows_first(k, middle)
        inner = columns(half_done[...], jnp.concatenate([cols_w[2], cols_w[2]], axis=0))
        for n in range(COMBOS):
            j, f = n // 5, n % 5
            means[PAIR * k + j, f] += inner[n * ROWS:(n + 1) * ROWS]
        for side in range(2):
            at = side * CX
            keep = (sub < 4) if side == 0 else (sub >= 4)

            def rows_of(j, f):
                return means[PAIR * k + j, f, pl.ds(at, 8)]

            last = rows_of(1, 1)
            for at_slot, (j, f) in enumerate(((0, 0), (0, 1), (1, 0))):
                spare = pltpu.roll(last, 6 - 2 * at_slot, 0)
                to_x[k, side, at_slot] = jnp.where(
                    (sub < 6) if side == 0 else (sub >= 2), rows_of(j, f), spare
                )
            for j in range(PAIR):
                to_x[k, side, 3 + j] = jnp.where(
                    keep, rows_of(j, 2), pltpu.roll(rows_of(j, 3), 4, 0)
                )
            to_x[k, side, 5] = jnp.where(keep, rows_of(0, 4), pltpu.roll(rows_of(1, 4), 4, 0))

    def middle_only(k, carry):
        middle_chunk(k)
        return carry

    def middle_and_send(k, carry):
        middle_chunk(k)
        for copy in sends_x(k):
            copy.start()
        return carry

    def send_only(k, carry):
        for copy in sends_x(k):
            copy.start()
        return carry

    ahead = AHEAD
    to_e[...] = jnp.zeros_like(to_e)
    lax.fori_loop(0, CHUNKS, side_chunk, 0)
    lax.fori_loop(0, ahead, middle_only, 0)
    pl.semaphore_wait(barrier, len(neighbours))
    for copy in sends_y():
        copy.start()
    lax.fori_loop(0, ahead, send_only, 0)
    lax.fori_loop(ahead, CHUNKS, middle_and_send, 0)

    for k in range(CHUNKS):
        for copy in sends_x(k):
            copy.wait()
    for copy in sends_y():
        copy.wait()


def filtered(east_flow, north_flow):
    dma = pltpu.SemaphoreType.DMA
    f32, bf16 = jnp.float32, jnp.bfloat16
    tiles = ROWS // 8
    shapes = (
        (LEV, 5, ROWS, CY), (CHUNKS, ROWS, CY),
        (2, tiles, CHUNKS * 8, CY), (4, CHUNKS * 8, CY), (CHUNKS, 2, TILES, 8, CY),
        (2, 8, CY),
    )
    return pl.pallas_call(
        filter_kernel,
        out_shape=tuple(jax.ShapeDtypeStruct(shape, f32) for shape in shapes),
        in_specs=[pl.BlockSpec(memory_space=pltpu.HBM)] * 4,
        out_specs=(pl.BlockSpec(memory_space=pltpu.VMEM),) * len(shapes),
        scratch_shapes=[
            pltpu.VMEM((2, LEV, FX, FY // 2), f32),
            pltpu.VMEM((2, LEV, FX, FY // 2), f32),
            pltpu.VMEM((2 * ROWS, 2 * FX), bf16),
            pltpu.VMEM((3, FY // 2, 2 * CY), bf16),
            pltpu.VMEM((COMBOS * ROWS, FY // 2), f32),
            pltpu.VMEM((2, tiles, CHUNKS * 8, CY), f32),
            pltpu.VMEM((CHUNKS, 2, TILES, 8, CY), f32),
            pltpu.VMEM((2, 8, CY), f32),
            dma((CHUNKS, 2, 3)),
            dma((2,)),
            dma((8,)),
            dma((8,)),
            dma((CHUNKS, 2)),
            dma((CHUNKS, 2)),
        ],
        compiler_params=pltpu.CompilerParams(
            collective_id=0, has_side_effects=True, vmem_limit_bytes=32 * 1024 * 1024
        ),
        name="filter_and_exchange",
    )(
        *[
            pltpu.with_memory_space_constraint(array, pltpu.HBM)
            for array in (
                east_flow, north_flow, jnp.asarray(row_factor()), jnp.asarray(column_factor())
            )
        ]
    )


def first_form(plus_two, plus_one, minus_one, minus_two):
    return (8.0 * (plus_one - minus_one) - (plus_two - minus_two)) * (1.0 / 12.0)


def second_form(plus_two, plus_one, centre, minus_one, minus_two):
    return (16.0 * (plus_one + minus_one) - (plus_two + minus_two) - 30.0 * centre) * (1.0 / 12.0)


def library_kernel(
    means, edges, from_y, from_c, from_x, from_e, stress, library, full, slopes, made_s, made_l, sem
):
    lane = lax.broadcasted_iota(jnp.int32, (ROWS, CY), 1)
    near = (lane % 8) >= 4
    sub = lax.broadcasted_iota(jnp.int32, (8, CY), 0)
    inside = (lane < 4) | (lane >= CY - 4)

    def stores(level):
        return (
            pltpu.make_async_copy(made_s.at[level], stress.at[:, level], sem.at[0, level]),
            pltpu.make_async_copy(made_l.at[level], library.at[:, level], sem.at[1, level]),
        )

    def ends(first, last):
        middle = jnp.zeros((CX - 8, CY), jnp.float32)
        return jnp.concatenate([first, middle, last], axis=0)

    def chunk(k, carry):
        at = pl.ds(8 * k, 8)
        from_left = from_y[0, :, at].reshape(ROWS, CY) + ends(from_c[1, at], from_c[0, at])
        from_right = from_y[1, :, at].reshape(ROWS, CY) + ends(from_c[3, at], from_c[2, at])
        back = lax.rem(CY - 32 * k, CY)
        own = edges[k] + ends(pltpu.roll(from_e[1], back, 1), pltpu.roll(from_e[0], back, 1))
        inward = jnp.where(near, from_left, from_right)
        outward = jnp.where(near, from_right, from_left) + own
        for j in range(PAIR):
            level = PAIR * k + j
            for f in range(5):
                if f < 2 and (j, f) != (1, 1):
                    first, last = from_x[k, 1, 2 * j + f], from_x[k, 0, 2 * j + f]
                elif f < 2:
                    first, last = [
                        jnp.where(
                            sub < low, pltpu.roll(from_x[k, side, 0], 2, 0),
                            jnp.where(
                                sub < low + 2, pltpu.roll(from_x[k, side, 1], 4, 0),
                                pltpu.roll(from_x[k, side, 2], 6, 0),
                            ),
                        )
                        for side, low in ((1, 4), (0, 2))
                    ]
                else:
                    slot = 3 + j if f < 4 else 5
                    first, last = from_x[k, 1, slot], from_x[k, 0, slot]
                    if f == 3 or (f == 4 and j == 1):
                        first, last = pltpu.roll(first, 4, 0), pltpu.roll(last, 4, 0)
                n = slot_of(j, f)
                full[f] = (
                    means[level, f]
                    + jnp.where(inside, turn(inward, -8 * n - 4), 0.0)
                    + ends(first, last)
                )
            results = []
            for f in range(2):
                field = full[f]
                rim = turn(outward, -8 * slot_of(j, f) - 4)
                side = [
                    turn(jnp.where(lane < 2, rim, field), -2),
                    turn(jnp.where(lane < 1, rim, field), -1),
                    turn(jnp.where(lane >= CY - 1, rim, field), 1),
                    turn(jnp.where(lane >= CY - 2, rim, field), 2),
                ]
                slopes[f] = first_form(*side)
                bend_y = second_form(side[0], side[1], field, side[2], side[3])[4:4 + CX]

                def row(step):
                    return full[f, pl.ds(4 + step, CX)]

                def slope_row(step):
                    return slopes[f, pl.ds(4 + step, CX)]

                centre = row(0)
                along = [row(2), row(1), row(-1), row(-2)]
                grad_x = first_form(*along)
                bend_x = second_form(along[0], along[1], centre, along[2], along[3])
                cross = first_form(slope_row(2), slope_row(1), slope_row(-1), slope_row(-2))
                results.append((centre, grad_x, slope_row(0), bend_x, cross, bend_y))
            east, ux, uy, uxx, uxy, uyy = results[0]
            north, vx, vy, vxx, vxy, vyy = results[1]
            made_s[level, 0] = full[2, pl.ds(4, CX)] - east * east
            made_s[level, 1] = full[3, pl.ds(4, CX)] - east * north
            made_s[level, 2] = full[4, pl.ds(4, CX)] - north * north
            spin = vx - uy
            features = [ux, uy, vx, vy, uxx, uxy, uyy, vxx, vxy, vyy, vxx - uxy, vxy - uyy]
            for n, feature in enumerate(features):
                made_l[level, 4 * n] = feature
                made_l[level, 4 * n + 1] = east * feature
                made_l[level, 4 * n + 2] = north * feature
                made_l[level, 4 * n + 3] = spin * feature
            for copy in stores(level):
                copy.start()
        return carry

    lax.fori_loop(0, CHUNKS, chunk, 0)

    def finish(level, carry):
        for copy in stores(level):
            copy.wait()
        return carry

    lax.fori_loop(0, LEV, finish, 0)


def outputs(*arrays):
    f32 = jnp.float32
    return pl.pallas_call(
        library_kernel,
        out_shape=(
            jax.ShapeDtypeStruct((3, LEV, CX, CY), f32),
            jax.ShapeDtypeStruct((48, LEV, CX, CY), f32),
        ),
        in_specs=[pl.BlockSpec(memory_space=pltpu.VMEM)] * len(arrays),
        out_specs=(pl.BlockSpec(memory_space=pltpu.HBM),) * 2,
        scratch_shapes=[
            pltpu.VMEM((5, ROWS, CY), f32),
            pltpu.VMEM((2, ROWS, CY), f32),
            pltpu.VMEM((LEV, 3, CX, CY), f32),
            pltpu.VMEM((LEV, 48, CX, CY), f32),
            pltpu.SemaphoreType.DMA((2, LEV)),
        ],
        compiler_params=pltpu.CompilerParams(vmem_limit_bytes=32 * 1024 * 1024),
        name="stress_and_library",
    )(*arrays)


def per_device(east_flow, north_flow):
    return outputs(*filtered(east_flow, north_flow))


def solution(mesh):
    return jax.shard_map(
        per_device,
        mesh=mesh,
        in_specs=(P(None, "gx", "gy"), P(None, "gx", "gy")),
        out_specs=(P(None, None, "gx", "gy"), P(None, None, "gx", "gy")),
        check_vma=False,
    )
```

```python
import jax
import jax.numpy as jnp
import ml_dtypes
import numpy as np
from jax import lax
from jax.experimental import pallas as pl
from jax.experimental.pallas import tpu as pltpu
from jax.sharding import PartitionSpec as P

spread_cells = 5.5
MESH = pl.DeviceIdType.MESH

LEV, FX, FY = 8, 128, 512
CX, CY = FX // 4, FY // 4
ROWS = CX + 8
PAIR = 2
CHUNKS = LEV // PAIR
COMBOS = 5 * PAIR
TILES = 6
AHEAD = 1


def slot_of(j, f):
    return 2 * j + f if f < 2 else 4 + 3 * j + f - 2


def gauss_taps():
    offsets = np.arange(33, dtype=np.float32) - np.float32(16.0)
    bumps = np.exp(np.float32(-0.5) * (offsets / np.float32(spread_cells)) ** 2)
    return (bumps / np.sum(bumps)).astype(np.float32)


def two_pieces(values):
    high = values.astype(ml_dtypes.bfloat16)
    low = (values - high.astype(np.float32)).astype(ml_dtypes.bfloat16)
    return high, low


def row_factor():
    taps = gauss_taps()
    band = np.zeros((ROWS, FX), np.float32)
    for at in range(ROWS):
        for p in range(FX):
            lag = p - 4 * (at - 4) + 16
            if 0 <= lag <= 32:
                band[at, p] = taps[lag]
    high, low = two_pieces(band)
    return np.concatenate(
        [np.concatenate([high, high], axis=1), np.concatenate([low, low], axis=1)], axis=0
    )


def column_factor():
    taps = gauss_taps()
    edge, half = FY // 4, FY // 2
    blocks = []
    for start, count in ((0, edge), (FY - edge, edge), (edge, half)):
        band = np.zeros((count, CY), np.float32)
        for c in range(-4, CY + 4):
            for p in range(count):
                lag = p + start - 4 * c + 16
                if 0 <= lag <= 32:
                    band[p, c % CY] = taps[lag]
        high, low = two_pieces(band)
        both = np.concatenate([high, low], axis=1)
        blocks.append(both if count == half else np.concatenate([both, both], axis=0))
    return np.stack(blocks, axis=0)


def split(values):
    high = values.astype(jnp.bfloat16)
    low = (values - high.astype(jnp.float32)).astype(jnp.bfloat16)
    return high, low


def turn(values, lanes):
    return pltpu.roll(values, lanes % CY, 1)


def filter_kernel(
    east, north, rows_hbm, cols_hbm, means, edges, from_y, from_c, from_x, from_e,
    sides, middle, rows_w, cols_w, half_done, to_y, to_x, to_e,
    load_sem, weight_sem, y_send, y_recv, x_send, x_recv,
):
    quarter = FY // 4

    def load(k, which, piece):
        source = (east if which == 0 else north).at[pl.ds(PAIR * k, PAIR)]
        levels = pl.ds(PAIR * k, PAIR)
        if piece == 0:
            source = source.at[:, :, pl.ds(0, quarter)]
            target = sides.at[which, levels, :, pl.ds(0, quarter)]
        elif piece == 1:
            source = source.at[:, :, pl.ds(3 * quarter, quarter)]
            target = sides.at[which, levels, :, pl.ds(quarter, quarter)]
        else:
            source = source.at[:, :, pl.ds(quarter, 2 * quarter)]
            target = middle.at[which, levels]
        return pltpu.make_async_copy(source, target, load_sem.at[k, which, piece])

    def start_loads(k, pieces):
        for which in range(2):
            for piece in pieces:
                load(k, which, piece).start()

    def wait_loads(k, pieces):
        for which in range(2):
            for piece in pieces:
                load(k, which, piece).wait()

    rows_copy = pltpu.make_async_copy(rows_hbm, rows_w, weight_sem.at[0])
    cols_copy = pltpu.make_async_copy(cols_hbm, cols_w, weight_sem.at[1])
    start_loads(0, (0, 1))
    rows_copy.start()
    cols_copy.start()
    here_x, here_y = lax.axis_index("gx"), lax.axis_index("gy")
    count_x, count_y = lax.axis_size("gx"), lax.axis_size("gy")
    up = jnp.where(here_x == count_x - 1, 0, here_x + 1)
    down = jnp.where(here_x == 0, count_x - 1, here_x - 1)
    right = jnp.where(here_y == count_y - 1, 0, here_y + 1)
    left = jnp.where(here_y == 0, count_y - 1, here_y - 1)
    corners = [(down, right), (up, right), (down, left), (up, left)]
    along_y = [(here_x, right), (here_x, left)]
    along_x = [(down, here_y), (up, here_y)]
    neighbours = corners + along_y + along_x

    barrier = pltpu.get_barrier_semaphore()
    for neighbour in neighbours:
        pl.semaphore_signal(barrier, inc=1, device_id=neighbour, device_id_type=MESH)

    for k in range(1, CHUNKS):
        start_loads(k, (0, 1))
    for k in range(CHUNKS):
        start_loads(k, (2,))

    def remote(source, target, send, recv, device):
        return pltpu.make_async_remote_copy(
            src_ref=source, dst_ref=target, send_sem=send, recv_sem=recv,
            device_id=device, device_id_type=MESH,
        )

    def sends_y():
        last = ROWS // 8 - 1
        pieces = [
            (to_y.at[0, 0], from_c.at[0]),
            (to_y.at[0, last], from_c.at[1]),
            (to_y.at[1, 0], from_c.at[2]),
            (to_y.at[1, last], from_c.at[3]),
            (to_y.at[0], from_y.at[0]),
            (to_y.at[1], from_y.at[1]),
            (to_e.at[0], from_e.at[0]),
            (to_e.at[1], from_e.at[1]),
        ]
        return [
            remote(source, target, y_send.at[n], y_recv.at[n], neighbours[n])
            for n, (source, target) in enumerate(pieces)
        ]

    def sends_x(k):
        return [
            remote(
                to_x.at[k, n], from_x.at[k, n], x_send.at[k, n], x_recv.at[k, n], along_x[n]
            )
            for n in range(2)
        ]

    rows_copy.wait()
    cols_copy.wait()

    lane = lax.broadcasted_iota(jnp.int32, (ROWS, CY), 1)
    group = lane // 8
    spot = lane % 8
    sub = lax.broadcasted_iota(jnp.int32, (8, CY), 0)

    def rows_first(k, fine):
        for j in range(PAIR):
            level = PAIR * k + j
            u = fine[0, level]
            v = fine[1, level]
            for f, values in enumerate((u, v, u * u, u * v, v * v)):
                high, low = split(values)
                both = jnp.dot(
                    rows_w[...], jnp.concatenate([high, low], axis=0),
                    preferred_element_type=jnp.float32,
                )
                half_done[pl.ds((5 * j + f) * ROWS, ROWS), :] = both[:ROWS] + both[ROWS:]

    def columns(values, weights):
        high, low = split(values)
        both = jnp.dot(
            jnp.concatenate([high, low], axis=1), weights, preferred_element_type=jnp.float32
        )
        return both[:, :CY] + both[:, CY:]

    def side_chunk(k, carry):
        wait_loads(k, (0, 1))
        rows_first(k, sides)
        from_low = columns(half_done[:, :quarter], cols_w[0])
        from_high = columns(half_done[:, quarter:], cols_w[1])
        packed_main = jnp.zeros((ROWS, CY), jnp.float32)
        packed_edge = jnp.zeros((ROWS, CY), jnp.float32)
        for at in range(COMBOS):
            j, f = at // 5, at % 5
            n = slot_of(j, f)
            first = from_low[at * ROWS:(at + 1) * ROWS]
            second = from_high[at * ROWS:(at + 1) * ROWS]
            main = jnp.where(lane < CY - 4, first, 0.0) + jnp.where(lane >= 4, second, 0.0)
            edge = jnp.where(lane >= CY // 2, first, second)
            means[PAIR * k + j, f] = main
            packed_edge = jnp.where(group == n, turn(edge, 8 * n + 4), packed_edge)
            if f < 2:
                packed_main = jnp.where(group == n, turn(main, 8 * n + 4), packed_main)
        edges[k] = packed_edge
        at = pl.ds(8 * k, 8)
        tiled = (ROWS // 8, 8, CY)
        quarter_lanes = lax.broadcasted_iota(jnp.int32, (8, CY), 1) // 32
        for side in range(2):
            turned = pltpu.roll(packed_edge[side * CX:side * CX + 8], 32 * k, 1)
            to_e[side] = jnp.where(quarter_lanes == k, turned, to_e[side])
        to_y[0, :, at] = jnp.where(spot >= 4, packed_edge, packed_main).reshape(tiled)
        to_y[1, :, at] = jnp.where(spot < 4, packed_edge, packed_main).reshape(tiled)
        return carry

    def middle_chunk(k):
        wait_loads(k, (2,))
        rows_first(k, middle)
        inner = columns(half_done[...], jnp.concatenate([cols_w[2], cols_w[2]], axis=0))
        for n in range(COMBOS):
            j, f = n // 5, n % 5
            means[PAIR * k + j, f] += inner[n * ROWS:(n + 1) * ROWS]
        for side in range(2):
            at = side * CX
            keep = (sub < 4) if side == 0 else (sub >= 4)

            def rows_of(j, f):
                return means[PAIR * k + j, f, pl.ds(at, 8)]

            last = rows_of(1, 1)
            for at_slot, (j, f) in enumerate(((0, 0), (0, 1), (1, 0))):
                spare = pltpu.roll(last, 6 - 2 * at_slot, 0)
                to_x[k, side, at_slot] = jnp.where(
                    (sub < 6) if side == 0 else (sub >= 2), rows_of(j, f), spare
                )
            for j in range(PAIR):
                to_x[k, side, 3 + j] = jnp.where(
                    keep, rows_of(j, 2), pltpu.roll(rows_of(j, 3), 4, 0)
                )
            to_x[k, side, 5] = jnp.where(keep, rows_of(0, 4), pltpu.roll(rows_of(1, 4), 4, 0))

    def middle_only(k, carry):
        middle_chunk(k)
        return carry

    def middle_and_send(k, carry):
        middle_chunk(k)
        for copy in sends_x(k):
            copy.start()
        return carry

    def send_only(k, carry):
        for copy in sends_x(k):
            copy.start()
        return carry

    ahead = AHEAD
    to_e[...] = jnp.zeros_like(to_e)
    lax.fori_loop(0, CHUNKS, side_chunk, 0)
    lax.fori_loop(0, ahead, middle_only, 0)
    pl.semaphore_wait(barrier, len(neighbours))
    copies = sends_y()
    for copy in copies[:4]:
        copy.start()
    lax.fori_loop(0, ahead, send_only, 0)
    for copy in copies[4:]:
        copy.start()
    lax.fori_loop(ahead, CHUNKS, middle_and_send, 0)

    for k in range(CHUNKS):
        for copy in sends_x(k):
            copy.wait()
    for copy in sends_y():
        copy.wait()


def filtered(east_flow, north_flow):
    dma = pltpu.SemaphoreType.DMA
    f32, bf16 = jnp.float32, jnp.bfloat16
    tiles = ROWS // 8
    shapes = (
        (LEV, 5, ROWS, CY), (CHUNKS, ROWS, CY),
        (2, tiles, CHUNKS * 8, CY), (4, CHUNKS * 8, CY), (CHUNKS, 2, TILES, 8, CY),
        (2, 8, CY),
    )
    return pl.pallas_call(
        filter_kernel,
        out_shape=tuple(jax.ShapeDtypeStruct(shape, f32) for shape in shapes),
        in_specs=[pl.BlockSpec(memory_space=pltpu.HBM)] * 4,
        out_specs=(pl.BlockSpec(memory_space=pltpu.VMEM),) * len(shapes),
        scratch_shapes=[
            pltpu.VMEM((2, LEV, FX, FY // 2), f32),
            pltpu.VMEM((2, LEV, FX, FY // 2), f32),
            pltpu.VMEM((2 * ROWS, 2 * FX), bf16),
            pltpu.VMEM((3, FY // 2, 2 * CY), bf16),
            pltpu.VMEM((COMBOS * ROWS, FY // 2), f32),
            pltpu.VMEM((2, tiles, CHUNKS * 8, CY), f32),
            pltpu.VMEM((CHUNKS, 2, TILES, 8, CY), f32),
            pltpu.VMEM((2, 8, CY), f32),
            dma((CHUNKS, 2, 3)),
            dma((2,)),
            dma((8,)),
            dma((8,)),
            dma((CHUNKS, 2)),
            dma((CHUNKS, 2)),
        ],
        compiler_params=pltpu.CompilerParams(
            collective_id=0, has_side_effects=True, vmem_limit_bytes=32 * 1024 * 1024
        ),
        name="filter_and_exchange",
    )(
        *[
            pltpu.with_memory_space_constraint(array, pltpu.HBM)
            for array in (
                east_flow, north_flow, jnp.asarray(row_factor()), jnp.asarray(column_factor())
            )
        ]
    )


def first_form(plus_two, plus_one, minus_one, minus_two):
    return (8.0 * (plus_one - minus_one) - (plus_two - minus_two)) * (1.0 / 12.0)


def second_form(plus_two, plus_one, centre, minus_one, minus_two):
    return (16.0 * (plus_one + minus_one) - (plus_two + minus_two) - 30.0 * centre) * (1.0 / 12.0)


def library_kernel(
    means, edges, from_y, from_c, from_x, from_e, stress, library, full, slopes, made_s, made_l, sem
):
    lane = lax.broadcasted_iota(jnp.int32, (ROWS, CY), 1)
    near = (lane % 8) >= 4
    sub = lax.broadcasted_iota(jnp.int32, (8, CY), 0)
    inside = (lane < 4) | (lane >= CY - 4)

    def stores(level):
        return (
            pltpu.make_async_copy(made_s.at[level], stress.at[:, level], sem.at[0, level]),
            pltpu.make_async_copy(made_l.at[level], library.at[:, level], sem.at[1, level]),
        )

    def ends(first, last):
        middle = jnp.zeros((CX - 8, CY), jnp.float32)
        return jnp.concatenate([first, middle, last], axis=0)

    def chunk(k, carry):
        at = pl.ds(8 * k, 8)
        from_left = from_y[0, :, at].reshape(ROWS, CY) + ends(from_c[1, at], from_c[0, at])
        from_right = from_y[1, :, at].reshape(ROWS, CY) + ends(from_c[3, at], from_c[2, at])
        back = lax.rem(CY - 32 * k, CY)
        own = edges[k] + ends(pltpu.roll(from_e[1], back, 1), pltpu.roll(from_e[0], back, 1))
        inward = jnp.where(near, from_left, from_right)
        outward = jnp.where(near, from_right, from_left) + own
        for j in range(PAIR):
            level = PAIR * k + j
            for f in range(5):
                if f < 2 and (j, f) != (1, 1):
                    first, last = from_x[k, 1, 2 * j + f], from_x[k, 0, 2 * j + f]
                elif f < 2:
                    first, last = [
                        jnp.where(
                            sub < low, pltpu.roll(from_x[k, side, 0], 2, 0),
                            jnp.where(
                                sub < low + 2, pltpu.roll(from_x[k, side, 1], 4, 0),
                                pltpu.roll(from_x[k, side, 2], 6, 0),
                            ),
                        )
                        for side, low in ((1, 4), (0, 2))
                    ]
                else:
                    slot = 3 + j if f < 4 else 5
                    first, last = from_x[k, 1, slot], from_x[k, 0, slot]
                    if f == 3 or (f == 4 and j == 1):
                        first, last = pltpu.roll(first, 4, 0), pltpu.roll(last, 4, 0)
                n = slot_of(j, f)
                full[f] = (
                    means[level, f]
                    + jnp.where(inside, turn(inward, -8 * n - 4), 0.0)
                    + ends(first, last)
                )
            results = []
            for f in range(2):
                field = full[f]
                rim = turn(outward, -8 * slot_of(j, f) - 4)
                side = [
                    turn(jnp.where(lane < 2, rim, field), -2),
                    turn(jnp.where(lane < 1, rim, field), -1),
                    turn(jnp.where(lane >= CY - 1, rim, field), 1),
                    turn(jnp.where(lane >= CY - 2, rim, field), 2),
                ]
                slopes[f] = first_form(*side)
                bend_y = second_form(side[0], side[1], field, side[2], side[3])[4:4 + CX]

                def row(step):
                    return full[f, pl.ds(4 + step, CX)]

                def slope_row(step):
                    return slopes[f, pl.ds(4 + step, CX)]

                centre = row(0)
                along = [row(2), row(1), row(-1), row(-2)]
                grad_x = first_form(*along)
                bend_x = second_form(along[0], along[1], centre, along[2], along[3])
                cross = first_form(slope_row(2), slope_row(1), slope_row(-1), slope_row(-2))
                results.append((centre, grad_x, slope_row(0), bend_x, cross, bend_y))
            east, ux, uy, uxx, uxy, uyy = results[0]
            north, vx, vy, vxx, vxy, vyy = results[1]
            made_s[level, 0] = full[2, pl.ds(4, CX)] - east * east
            made_s[level, 1] = full[3, pl.ds(4, CX)] - east * north
            made_s[level, 2] = full[4, pl.ds(4, CX)] - north * north
            spin = vx - uy
            features = [ux, uy, vx, vy, uxx, uxy, uyy, vxx, vxy, vyy, vxx - uxy, vxy - uyy]
            for n, feature in enumerate(features):
                made_l[level, 4 * n] = feature
                made_l[level, 4 * n + 1] = east * feature
                made_l[level, 4 * n + 2] = north * feature
                made_l[level, 4 * n + 3] = spin * feature
            for copy in stores(level):
                copy.start()
        return carry

    lax.fori_loop(0, CHUNKS, chunk, 0)

    def finish(level, carry):
        for copy in stores(level):
            copy.wait()
        return carry

    lax.fori_loop(0, LEV, finish, 0)


def outputs(*arrays):
    f32 = jnp.float32
    return pl.pallas_call(
        library_kernel,
        out_shape=(
            jax.ShapeDtypeStruct((3, LEV, CX, CY), f32),
            jax.ShapeDtypeStruct((48, LEV, CX, CY), f32),
        ),
        in_specs=[pl.BlockSpec(memory_space=pltpu.VMEM)] * len(arrays),
        out_specs=(pl.BlockSpec(memory_space=pltpu.HBM),) * 2,
        scratch_shapes=[
            pltpu.VMEM((5, ROWS, CY), f32),
            pltpu.VMEM((2, ROWS, CY), f32),
            pltpu.VMEM((LEV, 3, CX, CY), f32),
            pltpu.VMEM((LEV, 48, CX, CY), f32),
            pltpu.SemaphoreType.DMA((2, LEV)),
        ],
        compiler_params=pltpu.CompilerParams(vmem_limit_bytes=32 * 1024 * 1024),
        name="stress_and_library",
    )(*arrays)


def per_device(east_flow, north_flow):
    return outputs(*filtered(east_flow, north_flow))


def solution(mesh):
    return jax.shard_map(
        per_device,
        mesh=mesh,
        in_specs=(P(None, "gx", "gy"), P(None, "gx", "gy")),
        out_specs=(P(None, None, "gx", "gy"), P(None, None, "gx", "gy")),
        check_vma=False,
    )
```
